128 devices in a mesh: tp: 4 (over y_lo, core), dp: 32 (over x, z, y_hi).
Axes of the slice: x: 4, y: 4 (y_hi: 2, y_lo: 2; y = y_hi * 2 + y_lo), z: 4, core: 2. Of those that a mesh axis runs over, the one named last changes fastest.
Arguments:
- hidden: bfloat16 [32768, 7168], P('dp', 'tp'), may hold values from -6 to 6
- grad_out: bfloat16 [32768, 2048], P('dp', 'tp'), may hold values from -6 to 6
- momentum: bfloat16 [7168, 2048], P('tp'), may hold values from -6 to 6
- worker_err: bfloat16 [32, 7168, 2048], P('dp', 'tp'), may hold values from -6 to 6
- server_err: float32 [7168, 2048], P(('tp', 'dp')), may hold values from -6 to 6
Outputs:
- update: bfloat16 [7168, 2048], P('tp')
- corrected: float32 [7168, 2048], P(('tp', 'dp'))
The draws below stay inside these ranges and needn't reach their ends.
All inputs are finite; a program needn't handle non-finite values.
Results may differ from the reference program's by a relative error of at most 0.015.
Values may be sent and summed in bfloat16 or wider, within the bound.
No kernel may reach another device: no remote copies, remote signals or barrier semaphores. Data moves between devices by JAX's collectives and lax.ppermute only.
A program may use at most 192 MiB of HBM per device.

```python
import jax
import jax.numpy as jnp
from jax import lax

D = 2048
FF = 7168
TOK_DEV = 1024
BLOCK = 128
TOKENS = 32768
N_DP = 32


def with_spikes(values, own_key, source, target, blocks, factor):
    owner, partner = [(jnp.arange(values.shape[axis_at]) // (values.shape[axis_at] // blocks)).reshape([-1 if axis == axis_at else 1 for axis in range(values.ndim)]) for axis_at in (source, target)]
    chosen = jax.random.permutation(own_key, blocks)[partner]
    strong = (owner == chosen) | (owner == (partner + blocks // 2) % blocks)
    return jnp.where(strong, factor * values, values)


def shard_levels(stream_key, extent, split, smallest, top_value):
    loudness = 1.0
    for axis_at, shards_of in split:
        draws = jax.random.uniform(jax.random.fold_in(jax.random.fold_in(stream_key, 6), axis_at), (shards_of,), jnp.float32, smallest / len(split), top_value / len(split))
        loudness = loudness * jnp.repeat(jnp.exp(draws), extent[axis_at] // shards_of).reshape((-1,) + (1,) * (len(extent) - 1 - axis_at))
    return loudness


def centred(key, shape, spread, limit, split=(), kind=jnp.bfloat16):
    gain = shard_levels(key, shape, split, -0.22, 0.18) if split else 1.0
    values = jax.random.normal(key, shape, jnp.float32) * spread * gain
    return jnp.minimum(jnp.maximum(values, -limit), limit).astype(kind)


def heavy_noise(own_key, shape, deviation, bound, shards, heavy, kind=jnp.bfloat16):
    drawn = deviation * jax.random.normal(own_key, shape, jnp.float32)
    if shards:
        drawn = drawn * shard_levels(own_key, shape, shards, -0.22, 0.18)
    return jnp.clip(with_spikes(drawn, jax.random.fold_in(own_key, 3), *heavy), -bound, bound).astype(kind)


def setup_inputs(seed: int = 0) -> dict:
    key_of = jax.random.split(jax.random.key(seed), 6)
    return {
        "hidden": centred(key_of[0], (TOKENS, FF), 1.0, 6.0, ((0, 32), (1, 4))),
        "grad_out": centred(key_of[1], (TOKENS, D), (10 * N_DP ** 0.5 * TOK_DEV ** -0.5), 6.0, ((0, 32), (1, 4))),
        "momentum": centred(key_of[2], (FF, D), 1.0, 6.0, ((0, 4),)),
        "worker_err": heavy_noise(key_of[3], (N_DP, FF, D), 0.5, 6.0, ((0, 32), (1, 4)), (0, 1, 32, 2.75)),
        "server_err": centred(key_of[4], (FF, D), 0.5, 6.0, ((0, 128),), jnp.float32),
    }


clip_bound = 1.5

def compress(values):
    rows = values.shape[0]
    blocks = values.reshape(rows, values.shape[1] // BLOCK, BLOCK)
    scale = jnp.sqrt(lax.optimization_barrier(jnp.mean(blocks * blocks, axis=-1)) + 1e-06)
    codes = jnp.clip(blocks / scale[..., None], -clip_bound, clip_bound).astype(jnp.bfloat16)
    return (codes, scale)

def expand(codes, scale):
    rows = codes.shape[0]
    return (codes.astype(jnp.float32) * scale[..., None]).reshape(rows, -1)

def reference(hidden, grad_out, momentum, worker_err, server_err):
    shared = 0.9 * momentum.astype(jnp.float32)

    def replica(index, total):
        start = (index * TOK_DEV).astype(jnp.int32)
        acts = lax.dynamic_slice_in_dim(hidden, start, TOK_DEV, 0)
        cotan = lax.dynamic_slice_in_dim(grad_out, start, TOK_DEV, 0)
        grad = lax.dot_general(acts, cotan, (((0,), (0,)), ((), ())), preferred_element_type=jnp.float32)
        resid = lax.dynamic_index_in_dim(worker_err, index, 0, keepdims=False)
        values = shared + 0.1 * grad + resid.astype(jnp.float32)
        codes, scale = compress(values)
        return total + expand(codes, scale)
    total = lax.fori_loop(0, N_DP, replica, jnp.zeros((FF, D), jnp.float32))
    corrected = total / N_DP + server_err
    codes, scale = compress(corrected)
    update = expand(codes, scale).astype(jnp.bfloat16)
    return (update, corrected)
```

```python
import jax
import jax.numpy as jnp
from jax import lax
from jax.experimental import pallas as pl
from jax.experimental.pallas import tpu as pltpu
from jax.sharding import PartitionSpec as P

CLIP = 1.5
BLOCK = 128
WAYS = 4
GRAY = (0, 1, 3, 2)
ROW_TILE = 256
GROUP = 128
MIB = 1024 * 1024
F32 = jnp.float32
BF16 = jnp.bfloat16
AXES = ("tp", "dp")


def permute(array, phase, mask):
    pairs = []
    for tp in range(4):
        for x in range(4):
            for z in range(4):
                for half in range(2):
                    to_x, to_z, to_half = x, z, half
                    if phase == 2:
                        to_half = 1 - half
                    elif (tp + phase) % 2 == 0:
                        to_x = GRAY[GRAY[x] ^ mask]
                    else:
                        to_z = GRAY[GRAY[z] ^ mask]
                    pairs.append((tp * 32 + x * 8 + z * 2 + half, tp * 32 + to_x * 8 + to_z * 2 + to_half))
    return lax.ppermute(array, AXES, pairs)


def swap_tp(array, mask):
    return lax.ppermute(array, "tp", [(i, i ^ mask) for i in range(4)])


def clipped(part):
    square = jnp.sum(part * part, axis=1, keepdims=True) * (CLIP * CLIP / BLOCK) + CLIP * CLIP * 1e-06
    bound = square * lax.rsqrt(square)
    return jnp.clip(part, -bound, bound)


def coordinates():
    tp, dp = lax.axis_index("tp"), lax.axis_index("dp")
    return tp, dp // 8, (dp // 2) % 4, dp % 2


def ring_rows(first, second):
    tp, x, z, _ = coordinates()
    core = tp % 2
    on_x = first + core * (second - first)
    on_z = second + core * (first - second)
    code_x = x ^ (x >> 1) ^ on_x
    code_z = z ^ (z >> 1) ^ on_z
    return pl.multiple_of((code_x ^ (code_x >> 1)) * 448 + (code_z ^ (code_z >> 1)) * 112, 16)


def local_kernel(chunk, side, *refs):
    hidden, cotan, momentum, resid = refs[:4]
    send, keep, cross, values, grad = refs[-5:]
    depth, rows = hidden.shape
    width = cotan.shape[1]
    column = coordinates()[0] ^ (2 * chunk + side)

    def tile(hidden, momentum, resid):
        step = pl.program_id(0)
        grad[...] = jnp.dot(hidden[...].T, cotan[...], preferred_element_type=F32)

        def group(index, carry):
            at = pl.ds(pl.multiple_of(index * GROUP, GROUP), GROUP)
            to = pl.ds(pl.multiple_of(step * ROW_TILE + index * GROUP, GROUP), GROUP)
            for start in range(0, width, BLOCK):
                lanes = slice(start, start + BLOCK)
                total = 0.9 * momentum[at, lanes].astype(F32) + 0.1 * grad[at, lanes] + resid[at, lanes].astype(F32)
                values[to, lanes] = clipped(total).astype(BF16)
            return carry

        lax.fori_loop(0, ROW_TILE // GROUP, group, 0)

    pltpu.emit_pipeline(
        tile,
        grid=(rows // ROW_TILE,),
        in_specs=[
            pl.BlockSpec((depth, ROW_TILE), lambda i: (0, i)),
            pl.BlockSpec((ROW_TILE, width), lambda i: (i, column)),
            pl.BlockSpec((ROW_TILE, width), lambda i: (i, column)),
        ],
        out_specs=[],
    )(hidden, momentum, resid)

    for second in range(WAYS):
        for first in range(WAYS):
            piece = values[pl.ds(ring_rows(first, second), 112), :]
            if first == 0:
                keep[second] = piece
            elif first == 1 + side:
                send[0, second] = piece
            elif first == 2 - side:
                cross[second] = piece
            else:
                send[1, second] = piece


def local_values(chunk, side, hidden, cotan, momentum, resid, after):
    depth, rows = hidden.shape
    width = cotan.shape[1]
    out_shape = [shape(BF16, 2, WAYS, 112, width), shape(BF16, WAYS, 112, width), shape(BF16, WAYS, 112, width)]
    hbm, vmem = pl.BlockSpec(memory_space=pltpu.HBM), pl.BlockSpec(memory_space=pltpu.VMEM)
    return pl.pallas_call(
        lambda *refs: local_kernel(chunk, side, *refs),
        in_specs=[hbm, vmem, hbm, hbm] + [pl.BlockSpec(memory_space=pl.ANY)] * len(after),
        out_specs=[vmem] * 3,
        out_shape=out_shape,
        scratch_shapes=[pltpu.VMEM((rows, width), BF16), pltpu.VMEM((ROW_TILE, width), F32)],
        compiler_params=pltpu.CompilerParams(vmem_limit_bytes=12 * MIB),
        cost_estimate=pl.CostEstimate(
            flops=2 * rows * depth * width, bytes_accessed=2 * rows * (depth + 4 * width), transcendentals=0
        ),
        name="local_values",
    )(hidden, cotan, momentum, resid, *after)


def add(*terms):
    total = terms[0].astype(F32)
    for term in terms[1:]:
        total = total + term.astype(F32)
    return total


def small_call(kernel, name, out_shape, *args, after=()):
    count = len(args)
    moved = sum(a.size * a.dtype.itemsize for a in args) + sum(o.size * o.dtype.itemsize for o in out_shape)
    return pl.pallas_call(
        lambda *refs: kernel(*refs[:count], *refs[count + len(after) :]),
        in_specs=[pl.BlockSpec(memory_space=pltpu.VMEM)] * count + [pl.BlockSpec(memory_space=pl.ANY)] * len(after),
        out_specs=[pl.BlockSpec(memory_space=pltpu.VMEM)] * len(out_shape),
        out_shape=out_shape,
        compiler_params=pltpu.CompilerParams(vmem_limit_bytes=4 * MIB),
        cost_estimate=pl.CostEstimate(flops=moved, bytes_accessed=moved, transcendentals=0),
        name=name,
    )(*args, *after)


def shape(dtype, *dims):
    return jax.ShapeDtypeStruct(dims, dtype)


def forward_kernel(cross, got, out):
    out[...] = add(cross[...], got[1]).astype(BF16)


def ring_sum_kernel(keep0, keep1, r0, r1, u0, u1, *outs):
    width = keep0.shape[-1]
    for second, out in enumerate(outs):
        out[:, :width] = add(keep0[second], r0[0, second], u1[second]).astype(out.dtype)
        out[:, width:] = add(keep1[second], r1[0, second], u0[second]).astype(out.dtype)


def split_kernel(z0, w1, w2, w3, keep, send):
    total = add(z0[...], w1[...], w2[...], w3[...])
    low, high = total[:56], total[56:]
    is_low = coordinates()[3] == 0
    keep[...] = jnp.where(is_low, low, high)
    send[...] = jnp.where(is_low, high, low).astype(BF16)


def owner_kernel(keep, got, server, corrected, update):
    value = add(keep[...], got[...]) * (1.0 / 32) + server[...]
    corrected[...] = value
    for start in range(0, value.shape[1], BLOCK):
        lanes = slice(start, start + BLOCK)
        update[:, lanes] = clipped(value[:, lanes]).astype(BF16)


def pair_kernel(own, other, out):
    is_low = coordinates()[3] == 0
    out[:56] = jnp.where(is_low, own[...], other[...])
    out[56:] = jnp.where(is_low, other[...], own[...])


def stack_kernel(a, b, c, d, out0, out1):
    width = out0.shape[-1]
    for index, piece in enumerate((a, b, c, d)):
        out0[index] = piece[:, :width]
        out1[index] = piece[:, width:]


def place_kernel(pieces, *refs):
    count = len(pieces)
    out, sems = refs[-2:]
    tp = coordinates()[0]
    running = []
    for source, (first, chunk, side) in zip(refs[:count], pieces):
        width = source.shape[-1]
        columns = pl.ds(pl.multiple_of((tp ^ (2 * chunk + side)) * width, width), width)
        for second in range(WAYS):
            rows = pl.ds(ring_rows(first, second), 112)
            copy = pltpu.make_async_copy(source.at[second], out.at[rows, columns], sems.at[len(running)])
            copy.start()
            running.append(copy)
    for copy in running:
        copy.wait()


def place(pieces, arrays, rows, columns, so_far):
    chained = so_far is not None
    any_space = pl.BlockSpec(memory_space=pl.ANY)
    return pl.pallas_call(
        lambda *refs: place_kernel(pieces, *refs),
        in_specs=[pl.BlockSpec(memory_space=pltpu.VMEM)] * len(arrays) + [any_space] * chained,
        out_specs=any_space,
        out_shape=shape(BF16, rows, columns),
        scratch_shapes=[pltpu.SemaphoreType.DMA((WAYS * len(arrays),))],
        input_output_aliases={len(arrays): 0} if chained else {},
        compiler_params=pltpu.CompilerParams(vmem_limit_bytes=4 * MIB),
        cost_estimate=pl.CostEstimate(flops=0, bytes_accessed=arrays[0].size * 4 * len(arrays), transcendentals=0),
        name="place_update",
    )(*arrays, *((so_far,) if chained else ()))


class Chunk:
    def __init__(self, index, data, cotans):
        self.index, self.data, self.cotans = index, data, cotans
        self.rows, self.width = data[0].shape[1], cotans[0].shape[1]
        self.part = shape(BF16, WAYS, 112, self.width)
        self.held = {}

    def local(self, side, after):
        hidden, momentum, resid, _ = self.data
        send, keep, cross = local_values(self.index, side, hidden, self.cotans[side], momentum, resid, after)
        self.held[side] = (permute(send, 0, 1 + side), keep, cross)
        return cross

    def forward(self, side, after):
        got, _, _ = self.held[side]
        (out,) = small_call(forward_kernel, "forward", [self.part], self.held[side][2], got, after=after)
        self.held[side] += (permute(out, 0, 2 - side),)
        return out

    def ring_sum(self, after):
        (r0, keep0, _, u1), (r1, keep1, _, u0) = self.held[0], self.held[1]
        wide = [shape(t, 112, 2 * self.width) for t in (F32, BF16, BF16, BF16)]
        outs = small_call(ring_sum_kernel, "ring_sum", wide, keep0, keep1, r0, r1, u0, u1, after=after)
        self.sums = [outs[0]] + [permute(z, 1, mask) for mask, z in enumerate(outs) if mask]
        return outs[0]

    def split(self, after):
        out_shape = [shape(F32, 56, 2 * self.width), shape(BF16, 56, 2 * self.width)]
        self.kept, send = small_call(split_kernel, "split", out_shape, *self.sums, after=after)
        self.got = permute(send, 2, 0)
        return send

    def owner(self, after):
        tp = lax.axis_index("tp")
        server_err, width = self.data[3], self.width
        at = [(tp ^ (2 * self.index + side)) * width for side in (0, 1)]
        server = jnp.concatenate([lax.dynamic_slice_in_dim(server_err, a, width, 1) for a in at], 1)
        out_shape = [shape(F32, 56, 2 * width), shape(BF16, 56, 2 * width)]
        value, self.mine = small_call(owner_kernel, "owner", out_shape, self.kept, self.got, server, after=after)
        self.corrected = [(at[side], value[:, side * width : (side + 1) * width]) for side in (0, 1)]
        self.other = permute(self.mine, 2, 0)
        return self.mine

    def pair(self, after):
        (out,) = small_call(
            pair_kernel, "pair", [shape(BF16, 112, 2 * self.width)], self.mine, self.other, after=after
        )
        self.ring = [out] + [permute(out, 1, mask) for mask in (1, 2, 3)]
        return out

    def stack(self, after):
        own0, own1 = small_call(stack_kernel, "stack", [self.part, self.part], *self.ring, after=after)
        a0, b1 = permute(own0, 0, 1), permute(own1, 0, 2)
        b0, a1 = permute(own0, 0, 2), permute(own1, 0, 1)
        self.near = (own0, own1, a0, a1, b0, b1)
        self.far = (permute(a0, 0, 2), permute(b1, 0, 1))
        return own0

    def place(self, update, far):
        if far:
            return place([(3, self.index, 0), (3, self.index, 1)], self.far, self.rows, 4 * self.width, update)
        pieces = [(first, self.index, side) for first in (0, 1, 2) for side in (0, 1)]
        return place(pieces, self.near, self.rows, 4 * self.width, update)


def body(hidden, grad_out, momentum, worker_err, server_err):
    far = swap_tp(grad_out, 2)
    near = swap_tp(grad_out, 1)
    data = (hidden, momentum, worker_err[0], server_err)
    a = Chunk(0, data, (grad_out, near))
    b = Chunk(1, data, (far, swap_tp(far, 1)))
    last = ()
    for step in (
        lambda w: a.local(0, w),
        lambda w: a.local(1, w),
        lambda w: a.forward(0, w),
        lambda w: a.forward(1, w),
        lambda w: b.local(0, w),
        a.ring_sum,
        lambda w: b.local(1, w),
        a.split,
        lambda w: b.forward(0, w),
        a.owner,
        lambda w: b.forward(1, w),
        a.pair,
        b.ring_sum,
        a.stack,
        b.split,
        b.owner,
        b.pair,
        b.stack,
    ):
        last = (step(last),)
    update = a.place(None, False)
    update = a.place(update, True)
    update = b.place(update, False)
    update = b.place(update, True)
    whole = jnp.zeros(server_err.shape, F32)
    for at, value in a.corrected + b.corrected:
        whole = lax.dynamic_update_slice_in_dim(whole, value, at, 1)
    return (update, whole)


def solution(mesh):
    placed = (
        P("dp", "tp"),
        P("dp", "tp"),
        P("tp", None),
        P("dp", "tp", None),
        P(("tp", "dp"), None),
    )
    return jax.shard_map(
        body,
        mesh=mesh,
        in_specs=placed,
        out_specs=(P("tp", None), P(("tp", "dp"), None)),
        check_vma=False,
    )
```

```python
import jax
import jax.numpy as jnp
from jax import lax
from jax.experimental import pallas as pl
from jax.experimental.pallas import tpu as pltpu
from jax.sharding import PartitionSpec as P

CLIP = 1.5
BLOCK = 128
WAYS = 4
GRAY = (0, 1, 3, 2)
TILE = 448
GROUP = 64
LOCAL_MIB = 40
MIB = 1024 * 1024
F32 = jnp.float32
BF16 = jnp.bfloat16
AXES = ("tp", "dp")
COST_BYTES = 40000000
LOCAL_BYTES = 1000000


def permute(array, phase, mask):
    pairs = []
    for tp in range(4):
        for x in range(4):
            for z in range(4):
                for half in range(2):
                    to_x, to_z, to_half = x, z, half
                    if phase == 2:
                        to_half = 1 - half
                    elif (tp + phase) % 2 == 0:
                        to_x = GRAY[GRAY[x] ^ mask]
                    else:
                        to_z = GRAY[GRAY[z] ^ mask]
                    pairs.append((tp * 32 + x * 8 + z * 2 + half, tp * 32 + to_x * 8 + to_z * 2 + to_half))
    return lax.ppermute(array, AXES, pairs)


def swap_tp(array, mask):
    return lax.ppermute(array, "tp", [(i, i ^ mask) for i in range(4)])


def clipped(part):
    square = jnp.sum(part * part, axis=1, keepdims=True) * (CLIP * CLIP / BLOCK) + CLIP * CLIP * 1e-06
    bound = square * lax.rsqrt(square)
    return jnp.clip(part, -bound, bound)


def coordinates():
    tp, dp = lax.axis_index("tp"), lax.axis_index("dp")
    return tp, dp // 8, (dp // 2) % 4, dp % 2


def ring_rows(first, second):
    tp, x, z, _ = coordinates()
    core = tp % 2
    on_x = first + core * (second - first)
    on_z = second + core * (first - second)
    code_x = x ^ (x >> 1) ^ on_x
    code_z = z ^ (z >> 1) ^ on_z
    return pl.multiple_of((code_x ^ (code_x >> 1)) * 448 + (code_z ^ (code_z >> 1)) * 112, 16)


def local_kernel(chunk, sides, tile, *refs):
    count = len(sides)
    acts, momentum, resid = refs[:3]
    cotans = refs[3 : 3 + count]
    values, moments, resids, *grads, sems = refs[-6:]
    outs = refs[-6 - 3 * count : -6]
    turned = refs[-7 - 3 * count]
    rows, width = values.shape
    turn = acts.shape[0] == cotans[0].shape[0]
    steps = rows // tile
    running = []
    for index, side in enumerate(sides):
        column = pl.ds(pl.multiple_of((coordinates()[0] ^ (2 * chunk + side)) * width, width), width)
        for step in range(steps):
            at = pl.ds(step * tile, tile)
            copies = [
                pltpu.make_async_copy(momentum.at[at, column], moments.at[index, at], sems.at[index, 0, step]),
                pltpu.make_async_copy(resid.at[at, column], resids.at[index, at], sems.at[index, 1, step]),
            ]
            running.append(copies)
            for copy in copies:
                copy.start()

    def compress(index, step):
        for copy in running[index * steps + step]:
            copy.wait()
        grad = grads[step % 2]
        for low in range(0, tile, GROUP):
            at = slice(step * tile + low, step * tile + min(low + GROUP, tile))
            for start in range(0, width, BLOCK):
                lanes = slice(start, start + BLOCK)
                total = 0.9 * moments[index, at, lanes].astype(F32) + resids[index, at, lanes].astype(F32)
                total = total + 0.1 * grad[at.start - step * tile : at.stop - step * tile, lanes]
                values[at, lanes] = clipped(total).astype(BF16)

    for index, side in enumerate(sides):
        for step in range(steps):
            at = slice(step * tile, step * tile + tile)
            if turn:
                turned[at, :] = acts[:, at].T
                block = turned[at, :]
            else:
                block = acts[at, :]
            grads[step % 2][...] = jnp.dot(block, cotans[index][...], preferred_element_type=F32)
            if step:
                compress(index, step - 1)
        compress(index, steps - 1)

        send, keep, cross = outs[3 * index : 3 * index + 3]
        for second in range(WAYS):
            for first in range(WAYS):
                to = {0: keep, 1 + side: send.at[0], 2 - side: cross, 3: send.at[1]}[first]
                to[second] = values[pl.ds(ring_rows(first, second), 112), :]


def local_values(chunk, sides, acts, cotans, momentum, resid, after):
    depth, width = cotans[0].shape
    turn = acts.shape[0] == depth
    rows, count = momentum.shape[0], len(sides)
    tile = 256 if turn else TILE
    hbm, vmem = pl.BlockSpec(memory_space=pltpu.HBM), pl.BlockSpec(memory_space=pltpu.VMEM)
    part = shape(BF16, WAYS, 112, width)
    return pl.pallas_call(
        lambda *refs: local_kernel(chunk, sides, tile, *refs),
        in_specs=[vmem, hbm, hbm] + [vmem] * count + [pl.BlockSpec(memory_space=pl.ANY)] * len(after),
        out_specs=[vmem] * (3 * count + turn),
        out_shape=[shape(BF16, rows, depth)] * turn + [shape(BF16, 2, WAYS, 112, width), part, part] * count,
        scratch_shapes=[pltpu.VMEM((rows, width), BF16)]
        + [pltpu.VMEM((count, rows, width), BF16)] * 2
        + [pltpu.VMEM((tile, width), F32)] * 2
        + [pltpu.SemaphoreType.DMA((count, 2, rows // tile))],
        compiler_params=pltpu.CompilerParams(vmem_limit_bytes=LOCAL_MIB * MIB),
        cost_estimate=pl.CostEstimate(flops=0, bytes_accessed=LOCAL_BYTES, transcendentals=0),
        name="local_values",
    )(acts, momentum, resid, *cotans, *after)


def add(*terms):
    total = terms[0].astype(F32)
    for term in terms[1:]:
        total = total + term.astype(F32)
    return total


def small_call(kernel, name, out_shape, *args, after=()):
    count = len(args)
    return pl.pallas_call(
        lambda *refs: kernel(*refs[:count], *refs[count + len(after) :]),
        in_specs=[pl.BlockSpec(memory_space=pltpu.VMEM)] * count + [pl.BlockSpec(memory_space=pl.ANY)] * len(after),
        out_specs=[pl.BlockSpec(memory_space=pltpu.VMEM)] * len(out_shape),
        out_shape=out_shape,
        compiler_params=pltpu.CompilerParams(vmem_limit_bytes=4 * MIB),
        cost_estimate=pl.CostEstimate(flops=0, bytes_accessed=COST_BYTES, transcendentals=0),
        name=name,
    )(*args, *after)


def shape(dtype, *dims):
    return jax.ShapeDtypeStruct(dims, dtype)


def forward_kernel(*refs):
    count = len(refs) // 3
    for cross, got, out in zip(refs[:count], refs[count : 2 * count], refs[2 * count :]):
        out[...] = add(cross[...], got[1]).astype(BF16)


def ring_sum_kernel(keep0, keep1, r0, r1, u0, u1, *outs):
    width = keep0.shape[-1]
    for second, out in enumerate(outs):
        out[:, :width] = add(keep0[second], r0[0, second], u1[second]).astype(out.dtype)
        out[:, width:] = add(keep1[second], r1[0, second], u0[second]).astype(out.dtype)


def split_kernel(z0, w1, w2, w3, keep, send):
    total = add(z0[...], w1[...], w2[...], w3[...])
    low, high = total[:56], total[56:]
    is_low = coordinates()[3] == 0
    keep[...] = jnp.where(is_low, low, high)
    send[...] = jnp.where(is_low, high, low).astype(BF16)


def owner_kernel(chunk, keep, got, server, *refs):
    corrected, update = refs[-2:]
    half = keep.shape[1] // 2
    for side in (0, 1):
        column = pl.ds(pl.multiple_of((coordinates()[0] ^ (2 * chunk + side)) * half, half), half)
        lanes = slice(side * half, side * half + half)
        value = add(keep[:, lanes], got[:, lanes]) * (1.0 / 32) + server[:, column]
        corrected[:, column if chunk else lanes] = value
        if chunk:
            earlier = pl.ds(pl.multiple_of((coordinates()[0] ^ side) * half, half), half)
            corrected[:, earlier] = refs[0][:, lanes]
        for start in range(0, half, BLOCK):
            run = slice(side * half + start, side * half + start + BLOCK)
            update[:, run] = clipped(value[:, start : start + BLOCK]).astype(BF16)


def pair_kernel(own, other, out):
    is_low = coordinates()[3] == 0
    out[:56] = jnp.where(is_low, own[...], other[...])
    out[56:] = jnp.where(is_low, other[...], own[...])


def halves_kernel(got0, got1, out0, out1):
    width = out0.shape[-1]
    out0[...] = got0[:, :, :width]
    out1[...] = got1[:, :, width:]


def copy_kernel(source, out):
    out[...] = source[...]


def whole_stack_kernel(*refs):
    for index, piece in enumerate(refs[:-1]):
        refs[-1][index] = piece[...]


def stack_kernel(a, b, c, d, out0, out1):
    width = out0.shape[-1]
    for index, piece in enumerate((a, b, c, d)):
        out0[index] = piece[:, :width]
        out1[index] = piece[:, width:]


def place_kernel(pieces, *refs):
    out, sems = refs[-2:]
    tp = coordinates()[0]
    running = []
    for source, (first, chunk, sides) in zip(refs, pieces):
        width = source.shape[-1] // len(sides)
        for index, side in enumerate(sides):
            columns = pl.ds(pl.multiple_of((tp ^ (2 * chunk + side)) * width, width), width)
            for second in range(WAYS):
                rows = pl.ds(ring_rows(first, second), 112)
                piece = source.at[second, :, pl.ds(index * width, width)]
                copy = pltpu.make_async_copy(piece, out.at[rows, columns], sems.at[len(running)])
                copy.start()
                running.append(copy)
    for copy in running:
        copy.wait()


def place(pieces, arrays, rows, columns, so_far):
    chained = so_far is not None
    any_space = pl.BlockSpec(memory_space=pl.ANY)
    return pl.pallas_call(
        lambda *refs: place_kernel(pieces, *refs),
        in_specs=[pl.BlockSpec(memory_space=pltpu.VMEM)] * len(arrays) + [any_space] * chained,
        out_specs=any_space,
        out_shape=shape(BF16, rows, columns),
        scratch_shapes=[pltpu.SemaphoreType.DMA((WAYS * sum(len(p[2]) for p in pieces),))],
        input_output_aliases={len(arrays): 0} if chained else {},
        compiler_params=pltpu.CompilerParams(vmem_limit_bytes=4 * MIB),
        cost_estimate=pl.CostEstimate(flops=0, bytes_accessed=COST_BYTES, transcendentals=0),
        name="place_update",
    )(*arrays, *((so_far,) if chained else ()))


class Chunk:
    def __init__(self, index, data, cotans, gather):
        self.index, self.data, self.cotans, self.gather = index, data, cotans, gather
        self.rows, self.half = data[1].shape[0], cotans[0].shape[1]
        self.width = 2 * self.half
        self.part = shape(BF16, WAYS, 112, self.half)
        self.held = {}

    def local(self, sides, after):
        acts, momentum, resid, _ = self.data
        outs = local_values(self.index, sides, acts, [self.cotans[s] for s in sides], momentum, resid, after)
        if len(outs) == 3 * len(sides) + 1:
            self.data[0], *outs = outs
        for index, side in enumerate(sides):
            send, keep, cross = outs[3 * index : 3 * index + 3]
            self.held[side] = (permute(send, 0, 1 + side), keep, cross)
        return outs[-1]

    def forward(self, sides, after):
        held = [self.held[side] for side in sides]
        args = [cross for _, _, cross in held] + [got for got, _, _ in held]
        outs = small_call(forward_kernel, "forward", [self.part] * len(sides), *args, after=after)
        for side, out in zip(sides, outs):
            self.held[side] += (permute(out, 0, 2 - side),)
        return outs[0]

    def ring_sum(self, after):
        (r0, keep0, _, u1), (r1, keep1, _, u0) = self.held[0], self.held[1]
        wide = [shape(t, 112, self.width) for t in (F32, BF16, BF16, BF16)]
        outs = small_call(ring_sum_kernel, "ring_sum", wide, keep0, keep1, r0, r1, u0, u1, after=after)
        self.sums = [outs[0]] + [permute(outs[mask], 1, mask) for mask in (1, 2, 3)]
        return outs[0]

    def split(self, after):
        out_shape = [shape(F32, 56, self.width), shape(BF16, 56, self.width)]
        self.kept, send = small_call(split_kernel, "split", out_shape, *self.sums, after=after)
        self.got = permute(send, 2, 0)
        return send

    def owner(self, after, earlier=()):
        server_err = self.data[3]
        out_shape = [shape(F32, 56, server_err.shape[1] if earlier else self.width), shape(BF16, 56, self.width)]
        args = (self.kept, self.got, server_err, *earlier)
        kernel = lambda *refs: owner_kernel(self.index, *refs)
        self.value, self.mine = small_call(kernel, "owner", out_shape, *args, after=after)
        self.other = permute(self.mine, 2, 0)
        return self.mine

    def pair(self, after):
        out_shape = [shape(BF16, 112, self.width)]
        (out,) = small_call(pair_kernel, "pair", out_shape, self.mine, self.other, after=after)
        self.ring = [out] + [permute(out, 1, mask) for mask in (1, 2, 3)]
        return out

    def stack(self, after):
        if self.gather == "sides":
            own0, own1 = small_call(stack_kernel, "stack", [self.part, self.part], *self.ring, after=after)
            a0, b1 = permute(own0, 0, 1), permute(own1, 0, 2)
            b0, a1 = permute(own0, 0, 2), permute(own1, 0, 1)
            self.final = [[(0, own0, (0,)), (0, own1, (1,)), (1, a0, (0,)), (1, a1, (1,)), (2, b0, (0,)), (2, b1, (1,))]]
            self.final += [[(3, permute(a0, 0, 2), (0,)), (3, permute(b1, 0, 1), (1,))]]
            return own0
        whole = shape(BF16, WAYS, 112, self.width)
        (own,) = small_call(whole_stack_kernel, "stack", [whole], *self.ring, after=after)
        self.final = [[(0, own, (0, 1)), (1, permute(own, 0, 1), (0, 1)), (2, permute(own, 0, 2), (0, 1))]]
        if self.gather == "direct":
            self.final += [[(3, permute(own, 0, 3), (0, 1))]]
        return own

    def halves(self, after):
        a, b = self.final[0][1][1], self.final[0][2][1]
        left, right = small_call(halves_kernel, "halves", [self.part, self.part], a, b, after=after)
        self.final += [[(3, permute(left, 0, 2), (0,)), (3, permute(right, 0, 1), (1,))]]
        return left

    def place(self, update):
        for group in self.final:
            pieces = [(first, self.index, sides) for first, _, sides in group]
            update = place(pieces, [array for _, array, _ in group], self.rows, 2 * self.width, update)
        return update


GATHERS = ("sides", "sides")
ORDER = (
    "La0", "La1", "Fa0", "G", "Lb0", "Lb1", "Fb0", "Fa1", "Fb1", "Sa",
    "Sb", "Pa", "Pb", "Oa", "Ob", "Qa", "Qb", "Ka", "Kb",
)


def body(hidden, grad_out, momentum, worker_err, server_err):
    far = swap_tp(grad_out, 2)
    near = swap_tp(grad_out, 1)
    data = [hidden, momentum, worker_err[0], server_err]
    chunks = {"a": Chunk(0, data, (grad_out, near), GATHERS[0])}
    last = ()
    for word in ORDER:
        if word == "G":
            (far,) = small_call(copy_kernel, "take_far", [shape(BF16, *far.shape)], far, after=last)
            chunks["b"] = Chunk(1, data, (far, swap_tp(far, 1)), GATHERS[1])
            last = (far,)
            continue
        chunk, sides = chunks[word[1]], tuple(int(c) for c in word[2:])
        if word[0] == "L":
            out = chunk.local(sides, last)
        elif word[0] == "F":
            out = chunk.forward(sides, last)
        elif word[0] == "O":
            out = chunk.owner(last, (chunks["a"].value,) if word[1] == "b" else ())
        else:
            steps = {"S": chunk.ring_sum, "P": chunk.split, "Q": chunk.pair, "K": chunk.stack, "H": chunk.halves}
            out = steps[word[0]](last)
        last = (out,)
    update = chunks["b"].place(chunks["a"].place(None))
    return (update, chunks["b"].value)


def solution(mesh):
    placed = (
        P("dp", "tp"),
        P("dp", "tp"),
        P("tp", None),
        P("dp", "tp", None),
        P(("tp", "dp"), None),
    )
    return jax.shard_map(
        body,
        mesh=mesh,
        in_specs=placed,
        out_specs=(P("tp", None), P(("tp", "dp"), None)),
        check_vma=False,
    )
```

```python
import jax
import jax.numpy as jnp
from jax import lax
from jax.experimental import pallas as pl
from jax.experimental.pallas import tpu as pltpu
from jax.sharding import PartitionSpec as P

CLIP = 1.5
BLOCK = 128
WAYS = 4
GRAY = (0, 1, 3, 2)
TILE = 448
GROUP = 64
LOCAL_MIB = 40
MIB = 1024 * 1024
F32 = jnp.float32
BF16 = jnp.bfloat16
AXES = ("tp", "dp")
COST_BYTES = 40000000
LOCAL_BYTES = 1000000


def permute(array, phase, mask):
    pairs = []
    for tp in range(4):
        for x in range(4):
            for z in range(4):
                for half in range(2):
                    to_x, to_z, to_half = x, z, half
                    if phase == 2:
                        to_half = 1 - half
                    elif (tp + phase) % 2 == 0:
                        to_x = GRAY[GRAY[x] ^ mask]
                    else:
                        to_z = GRAY[GRAY[z] ^ mask]
                    pairs.append((tp * 32 + x * 8 + z * 2 + half, tp * 32 + to_x * 8 + to_z * 2 + to_half))
    return lax.ppermute(array, AXES, pairs)


def swap_tp(array, mask):
    return lax.ppermute(array, "tp", [(i, i ^ mask) for i in range(4)])


def clipped(part):
    square = jnp.sum(part * part, axis=1, keepdims=True) * (CLIP * CLIP / BLOCK) + CLIP * CLIP * 1e-06
    bound = square * lax.rsqrt(square)
    return jnp.clip(part, -bound, bound)


def coordinates():
    tp, dp = lax.axis_index("tp"), lax.axis_index("dp")
    return tp, dp // 8, (dp // 2) % 4, dp % 2


def ring_rows(first, second):
    tp, x, z, _ = coordinates()
    core = tp % 2
    on_x = first + core * (second - first)
    on_z = second + core * (first - second)
    code_x = x ^ (x >> 1) ^ on_x
    code_z = z ^ (z >> 1) ^ on_z
    return pl.multiple_of((code_x ^ (code_x >> 1)) * 448 + (code_z ^ (code_z >> 1)) * 112, 16)


def local_kernel(chunk, sides, tile, *refs):
    count = len(sides)
    acts, momentum, resid = refs[:3]
    cotans = refs[3 : 3 + count]
    values, moments, resids, *grads, sems = refs[-6:]
    outs = refs[-6 - 3 * count : -6]
    turned = refs[-7 - 3 * count]
    rows, width = values.shape
    turn = acts.shape[0] == cotans[0].shape[0]
    steps = rows // tile
    running = []
    for index, side in enumerate(sides):
        column = pl.ds(pl.multiple_of((coordinates()[0] ^ (2 * chunk + side)) * width, width), width)
        for step in range(steps):
            at = pl.ds(step * tile, tile)
            copies = [
                pltpu.make_async_copy(momentum.at[at, column], moments.at[index, at], sems.at[index, 0, step]),
                pltpu.make_async_copy(resid.at[at, column], resids.at[index, at], sems.at[index, 1, step]),
            ]
            running.append(copies)
            for copy in copies:
                copy.start()

    def compress(index, step):
        for copy in running[index * steps + step]:
            copy.wait()
        grad = grads[step % 2]
        for low in range(0, tile, GROUP):
            at = slice(step * tile + low, step * tile + min(low + GROUP, tile))
            for start in range(0, width, BLOCK):
                lanes = slice(start, start + BLOCK)
                total = 0.9 * moments[index, at, lanes].astype(F32) + resids[index, at, lanes].astype(F32)
                total = total + 0.1 * grad[at.start - step * tile : at.stop - step * tile, lanes]
                values[at, lanes] = clipped(total).astype(BF16)

    for index, side in enumerate(sides):
        for step in range(steps):
            at = slice(step * tile, step * tile + tile)
            if turn:
                turned[at, :] = acts[:, at].T
                block = turned[at, :]
            else:
                block = acts[at, :]
            grads[step % 2][...] = jnp.dot(block, cotans[index][...], preferred_element_type=F32)
            if step:
                compress(index, step - 1)
        compress(index, steps - 1)

        send, keep, cross = outs[3 * index : 3 * index + 3]
        for second in range(WAYS):
            for first in range(WAYS):
                to = {0: keep, 1 + side: send.at[0], 2 - side: cross, 3: send.at[1]}[first]
                to[second] = values[pl.ds(ring_rows(first, second), 112), :]


def local_values(chunk, sides, acts, cotans, momentum, resid, after):
    depth, width = cotans[0].shape
    turn = acts.shape[0] == depth
    rows, count = momentum.shape[0], len(sides)
    tile = 256 if turn else TILE
    hbm, vmem = pl.BlockSpec(memory_space=pltpu.HBM), pl.BlockSpec(memory_space=pltpu.VMEM)
    part = shape(BF16, WAYS, 112, width)
    return pl.pallas_call(
        lambda *refs: local_kernel(chunk, sides, tile, *refs),
        in_specs=[vmem, hbm, hbm] + [vmem] * count + [pl.BlockSpec(memory_space=pl.ANY)] * len(after),
        out_specs=[vmem] * (3 * count + turn),
        out_shape=[shape(BF16, rows, depth)] * turn + [shape(BF16, 2, WAYS, 112, width), part, part] * count,
        scratch_shapes=[pltpu.VMEM((rows, width), BF16)]
        + [pltpu.VMEM((count, rows, width), BF16)] * 2
        + [pltpu.VMEM((tile, width), F32)] * 2
        + [pltpu.SemaphoreType.DMA((count, 2, rows // tile))],
        compiler_params=pltpu.CompilerParams(vmem_limit_bytes=LOCAL_MIB * MIB),
        cost_estimate=pl.CostEstimate(flops=0, bytes_accessed=LOCAL_BYTES, transcendentals=0),
        name="local_values",
    )(acts, momentum, resid, *cotans, *after)


def add(*terms):
    total = terms[0].astype(F32)
    for term in terms[1:]:
        total = total + term.astype(F32)
    return total


def small_call(kernel, name, out_shape, *args, after=()):
    count = len(args)
    return pl.pallas_call(
        lambda *refs: kernel(*refs[:count], *refs[count + len(after) :]),
        in_specs=[pl.BlockSpec(memory_space=pltpu.VMEM)] * count + [pl.BlockSpec(memory_space=pl.ANY)] * len(after),
        out_specs=[pl.BlockSpec(memory_space=pltpu.VMEM)] * len(out_shape),
        out_shape=out_shape,
        compiler_params=pltpu.CompilerParams(vmem_limit_bytes=4 * MIB),
        cost_estimate=pl.CostEstimate(flops=0, bytes_accessed=COST_BYTES, transcendentals=0),
        name=name,
    )(*args, *after)


def shape(dtype, *dims):
    return jax.ShapeDtypeStruct(dims, dtype)


def forward_kernel(*refs):
    count = len(refs) // 3
    for cross, got, out in zip(refs[:count], refs[count : 2 * count], refs[2 * count :]):
        out[...] = add(cross[...], got[1]).astype(BF16)


def ring_sum_kernel(keep0, keep1, r0, r1, u0, u1, *outs):
    width = keep0.shape[-1]
    for second, out in enumerate(outs):
        out[:, :width] = add(keep0[second], r0[0, second], u1[second]).astype(out.dtype)
        out[:, width:] = add(keep1[second], r1[0, second], u0[second]).astype(out.dtype)


def split_kernel(z0, w1, w2, w3, keep, send):
    total = add(z0[...], w1[...], w2[...], w3[...])
    low, high = total[:56], total[56:]
    is_low = coordinates()[3] == 0
    keep[...] = jnp.where(is_low, low, high)
    send[...] = jnp.where(is_low, high, low).astype(BF16)


def owner_kernel(chunk, keep, got, server, *refs):
    corrected, update = refs[-2:]
    half = keep.shape[1] // 2
    for side in (0, 1):
        column = pl.ds(pl.multiple_of((coordinates()[0] ^ (2 * chunk + side)) * half, half), half)
        lanes = slice(side * half, side * half + half)
        value = add(keep[:, lanes], got[:, lanes]) * (1.0 / 32) + server[:, column]
        corrected[:, column if chunk else lanes] = value
        if chunk:
            earlier = pl.ds(pl.multiple_of((coordinates()[0] ^ side) * half, half), half)
            corrected[:, earlier] = refs[0][:, lanes]
        for start in range(0, half, BLOCK):
            run = slice(side * half + start, side * half + start + BLOCK)
            update[:, run] = clipped(value[:, start : start + BLOCK]).astype(BF16)


def pair_kernel(own, other, out):
    is_low = coordinates()[3] == 0
    out[:56] = jnp.where(is_low, own[...], other[...])
    out[56:] = jnp.where(is_low, other[...], own[...])


def halves_kernel(got0, got1, out0, out1):
    width = out0.shape[-1]
    out0[...] = got0[:, :, :width]
    out1[...] = got1[:, :, width:]


def copy_kernel(source, out):
    out[...] = source[...]


def whole_stack_kernel(*refs):
    for index, piece in enumerate(refs[:-1]):
        refs[-1][index] = piece[...]


def stack_kernel(a, b, c, d, out0, out1):
    width = out0.shape[-1]
    for index, piece in enumerate((a, b, c, d)):
        out0[index] = piece[:, :width]
        out1[index] = piece[:, width:]


def place_kernel(pieces, *refs):
    out, sems = refs[-2:]
    tp = coordinates()[0]
    running = []
    for source, (first, chunk, sides) in zip(refs, pieces):
        width = source.shape[-1] // len(sides)
        for index, side in enumerate(sides):
            columns = pl.ds(pl.multiple_of((tp ^ (2 * chunk + side)) * width, width), width)
            for second in range(WAYS):
                rows = pl.ds(ring_rows(first, second), 112)
                piece = source.at[second, :, pl.ds(index * width, width)]
                copy = pltpu.make_async_copy(piece, out.at[rows, columns], sems.at[len(running)])
                copy.start()
                running.append(copy)
    for copy in running:
        copy.wait()


def place(pieces, arrays, rows, columns, so_far):
    chained = so_far is not None
    any_space = pl.BlockSpec(memory_space=pl.ANY)
    return pl.pallas_call(
        lambda *refs: place_kernel(pieces, *refs),
        in_specs=[pl.BlockSpec(memory_space=pltpu.VMEM)] * len(arrays) + [any_space] * chained,
        out_specs=any_space,
        out_shape=shape(BF16, rows, columns),
        scratch_shapes=[pltpu.SemaphoreType.DMA((WAYS * sum(len(p[2]) for p in pieces),))],
        input_output_aliases={len(arrays): 0} if chained else {},
        compiler_params=pltpu.CompilerParams(vmem_limit_bytes=4 * MIB),
        cost_estimate=pl.CostEstimate(flops=0, bytes_accessed=COST_BYTES, transcendentals=0),
        name="place_update",
    )(*arrays, *((so_far,) if chained else ()))


class Chunk:
    def __init__(self, index, data, cotans, gather):
        self.index, self.data, self.cotans, self.gather = index, data, cotans, gather
        self.rows, self.half = data[1].shape[0], cotans[0].shape[1]
        self.width = 2 * self.half
        self.part = shape(BF16, WAYS, 112, self.half)
        self.held = {}

    def local(self, sides, after):
        acts, momentum, resid, _ = self.data
        outs = local_values(self.index, sides, acts, [self.cotans[s] for s in sides], momentum, resid, after)
        if len(outs) == 3 * len(sides) + 1:
            self.data[0], *outs = outs
        for index, side in enumerate(sides):
            send, keep, cross = outs[3 * index : 3 * index + 3]
            self.held[side] = (permute(send, 0, 1 + side), keep, cross)
        return outs[-1]

    def forward(self, sides, after):
        held = [self.held[side] for side in sides]
        args = [cross for _, _, cross in held] + [got for got, _, _ in held]
        outs = small_call(forward_kernel, "forward", [self.part] * len(sides), *args, after=after)
        for side, out in zip(sides, outs):
            self.held[side] += (permute(out, 0, 2 - side),)
        return outs[0]

    def ring_sum(self, after):
        (r0, keep0, _, u1), (r1, keep1, _, u0) = self.held[0], self.held[1]
        wide = [shape(t, 112, self.width) for t in (F32, BF16, BF16, BF16)]
        outs = small_call(ring_sum_kernel, "ring_sum", wide, keep0, keep1, r0, r1, u0, u1, after=after)
        self.sums = [outs[0]] + [permute(outs[mask], 1, mask) for mask in (1, 2, 3)]
        return outs[0]

    def split(self, after):
        out_shape = [shape(F32, 56, self.width), shape(BF16, 56, self.width)]
        self.kept, send = small_call(split_kernel, "split", out_shape, *self.sums, after=after)
        self.got = permute(send, 2, 0)
        return send

    def owner(self, after, earlier=()):
        server_err = self.data[3]
        out_shape = [shape(F32, 56, server_err.shape[1] if earlier else self.width), shape(BF16, 56, self.width)]
        args = (self.kept, self.got, server_err, *earlier)
        kernel = lambda *refs: owner_kernel(self.index, *refs)
        self.value, self.mine = small_call(kernel, "owner", out_shape, *args, after=after)
        self.other = permute(self.mine, 2, 0)
        return self.mine

    def pair(self, after):
        out_shape = [shape(BF16, 112, self.width)]
        (out,) = small_call(pair_kernel, "pair", out_shape, self.mine, self.other, after=after)
        self.ring = [out] + [permute(out, 1, mask) for mask in (1, 2, 3)]
        return out

    def stack(self, after):
        if self.gather == "sides":
            own0, own1 = small_call(stack_kernel, "stack", [self.part, self.part], *self.ring, after=after)
            a0, b1 = permute(own0, 0, 1), permute(own1, 0, 2)
            b0, a1 = permute(own0, 0, 2), permute(own1, 0, 1)
            self.final = [[(0, own0, (0,)), (0, own1, (1,)), (1, a0, (0,)), (1, a1, (1,)), (2, b0, (0,)), (2, b1, (1,))]]
            self.final += [[(3, permute(a0, 0, 2), (0,)), (3, permute(b1, 0, 1), (1,))]]
            return own0
        whole = shape(BF16, WAYS, 112, self.width)
        (own,) = small_call(whole_stack_kernel, "stack", [whole], *self.ring, after=after)
        self.final = [[(0, own, (0, 1)), (1, permute(own, 0, 1), (0, 1)), (2, permute(own, 0, 2), (0, 1))]]
        if self.gather == "direct":
            self.final += [[(3, permute(own, 0, 3), (0, 1))]]
        return own

    def halves(self, after):
        a, b = self.final[0][1][1], self.final[0][2][1]
        left, right = small_call(halves_kernel, "halves", [self.part, self.part], a, b, after=after)
        self.final += [[(3, permute(left, 0, 2), (0,)), (3, permute(right, 0, 1), (1,))]]
        return left

    def place(self, update):
        for group in self.final:
            pieces = [(first, self.index, sides) for first, _, sides in group]
            update = place(pieces, [array for _, array, _ in group], self.rows, 2 * self.width, update)
        return update


GATHERS = ("sides", "sides")
ORDER = (
    "La0", "La1", "Fa01", "G", "Lb0", "Lb1", "Fb0", "Fb1", "Sa", "Sb",
    "Pa", "Pb", "Oa", "Ob", "Qa", "Qb", "Ka", "Kb",
)


def body(hidden, grad_out, momentum, worker_err, server_err):
    far = swap_tp(grad_out, 2)
    near = swap_tp(grad_out, 1)
    data = [hidden, momentum, worker_err[0], server_err]
    chunks = {"a": Chunk(0, data, (grad_out, near), GATHERS[0])}
    last = ()
    for word in ORDER:
        if word == "G":
            (far,) = small_call(copy_kernel, "take_far", [shape(BF16, *far.shape)], far, after=last)
            chunks["b"] = Chunk(1, data, (far, swap_tp(far, 1)), GATHERS[1])
            last = (far,)
            continue
        chunk, sides = chunks[word[1]], tuple(int(c) for c in word[2:])
        if word[0] == "L":
            out = chunk.local(sides, last)
        elif word[0] == "F":
            out = chunk.forward(sides, last)
        elif word[0] == "O":
            out = chunk.owner(last, (chunks["a"].value,) if word[1] == "b" else ())
        else:
            steps = {"S": chunk.ring_sum, "P": chunk.split, "Q": chunk.pair, "K": chunk.stack, "H": chunk.halves}
            out = steps[word[0]](last)
        last = (out,)
    update = chunks["b"].place(chunks["a"].place(None))
    return (update, chunks["b"].value)


def solution(mesh):
    placed = (
        P("dp", "tp"),
        P("dp", "tp"),
        P("tp", None),
        P("dp", "tp", None),
        P(("tp", "dp"), None),
    )
    return jax.shard_map(
        body,
        mesh=mesh,
        in_specs=placed,
        out_specs=(P("tp", None), P(("tp", "dp"), None)),
        check_vma=False,
    )
```
